128 devices in a mesh: inp: 32 (over z_lo, x, y), tim: 4 (over z_hi, core).
Axes of the slice: x: 4, y: 4, z: 4 (z_hi: 2, z_lo: 2; z = z_hi * 2 + z_lo), core: 2. Of those that a mesh axis runs over, the one named last changes fastest.
Arguments:
- voltages: bfloat16 [1024, 524288], P('inp', 'tim'), may hold values from -6 to 6
Outputs:
- visibility: float32 [256, 2, 1024, 1024], P(('inp', 'tim'))
The draws below stay inside these ranges and needn't reach their ends.
All inputs are finite; a program needn't handle non-finite values.
Results may differ from the reference program's by a relative error of at most 0.0063.
Values may be sent and summed in bfloat16 or wider, within the bound.
A program may use at most 128 MiB of HBM per device.

```python
import math
import jax
import jax.numpy as jnp
from jax import lax

INPUTS = 1024
NFFT = 2048
TAPS = 4
CH0 = 384
CHAN = 256
FRAMES = 256


def steps_of(own_key, shape, shards, low, largest):
    def one(position, blocks):
        heights = jax.random.uniform(jax.random.fold_in(jax.random.fold_in(own_key, 6), position), (blocks,), jnp.float32, low / len(shards), largest / len(shards))
        return jnp.repeat(jnp.exp(heights), shape[position] // blocks).reshape((-1,) + (1,) * (len(shape) - position - 1))

    loudness = one(*shards[0])
    for cut in shards[1:]:
        loudness = loudness * one(*cut)
    return loudness


def noise(own_key, dims, width, most, pieces=(), held_as=jnp.bfloat16):
    array = width * jax.random.normal(own_key, dims, jnp.float32)
    if pieces:
        array = array * steps_of(own_key, dims, pieces, -0.22, 0.18)
    return jnp.clip(array, -most, most).astype(held_as)


def setup_inputs(seed: int = 0) -> dict:
    streams_of = jax.random.split(jax.random.key(seed), 2)
    return {
        "voltages": noise(streams_of[0], (INPUTS, FRAMES * NFFT), 1.0, 6.0, ((0, 32), (1, 4))),
    }


def filter_window(length, taps):
    places = jnp.arange(taps * length).astype(jnp.float32)
    span_total = taps * length
    centred = (places - span_total / 2 + 0.5) / length
    taper = 0.5 - 0.5 * jnp.cos(2.0 * math.pi * (places + 0.5) / span_total)
    return (jnp.sinc(centred) * taper).reshape(taps, length)

def channel_table(length, first, count):
    samples = jnp.arange(length).astype(jnp.int32)
    channels = (first + jnp.arange(count)).astype(jnp.int32)
    phase = samples[:, None] * channels[None, :] % length
    angle = phase.astype(jnp.float32) * (2.0 * math.pi / length)
    scaling = 1.0 / math.sqrt(length)
    return jnp.concatenate([jnp.cos(angle) * scaling, -jnp.sin(angle) * scaling], axis=1).astype(jnp.bfloat16)

def reference(voltages):
    window = filter_window(NFFT, TAPS)
    table = channel_table(NFFT, CH0, CHAN)
    block_rows = 32 if INPUTS % 32 == 0 else INPUTS
    grouped = voltages.reshape(INPUTS // block_rows, block_rows, FRAMES * NFFT)

    def transform(block):
        padded = jnp.concatenate([block, jnp.zeros((block_rows, (TAPS - 1) * NFFT), jnp.bfloat16)], axis=1)
        stream = padded.reshape(block_rows, FRAMES + TAPS - 1, NFFT).astype(jnp.float32)
        summed = jnp.zeros((block_rows, FRAMES, NFFT), jnp.float32)
        for tap_index in range(TAPS):
            summed = summed + window[tap_index][None, None, :] * stream[:, tap_index:tap_index + FRAMES, :]
        filtered = summed.astype(jnp.bfloat16)
        spectra = jnp.dot(filtered.reshape(block_rows * FRAMES, NFFT), table, preferred_element_type=jnp.float32)
        return spectra.astype(jnp.bfloat16).reshape(block_rows, FRAMES, 2, CHAN)
    spectra = lax.map(transform, grouped).reshape(INPUTS, FRAMES, 2, CHAN)
    by_channel = jnp.transpose(spectra, (3, 2, 0, 1))

    def correlate(parts):
        real_part = parts[0].astype(jnp.float32)
        imag_part = parts[1].astype(jnp.float32)
        joined_parts = jnp.concatenate([real_part, imag_part], axis=1)
        rotated = jnp.concatenate([imag_part, -real_part], axis=1)
        stacked = jnp.concatenate([joined_parts, rotated], axis=0)
        product = jnp.dot(stacked, joined_parts.T, precision=lax.Precision.HIGHEST, preferred_element_type=jnp.float32)
        return (product * (1.0 / FRAMES)).reshape(2, INPUTS, INPUTS)
    return lax.map(correlate, by_channel)
```

```python
import functools
import math

import jax
import jax.numpy as jnp
import numpy as np
from jax import lax
from jax.experimental import pallas as pl
from jax.experimental.pallas import tpu as pltpu
from jax.sharding import PartitionSpec as P

NFFT = 2048
TAPS = 4
CH0 = 384
CHAN = 256
MESH = pl.DeviceIdType.MESH
ROWS = 16
LANES = 128
GROUP = 16
STRIDE = 45


def filter_window():
    span = TAPS * NFFT
    places = np.arange(span).astype(np.float32)
    centred = (places - np.float32(span / 2) + np.float32(0.5)) / np.float32(NFFT)
    taper = 0.5 - 0.5 * np.cos(2.0 * math.pi * (places + 0.5) / span)
    return (np.sinc(centred.astype(np.float64)) * taper).astype(np.float32).reshape(TAPS, NFFT)


def table():
    samples = np.arange(NFFT)
    channels = CH0 + np.arange(CHAN)
    angle = (samples[:, None] * channels[None, :] % NFFT) * (2.0 * math.pi / NFFT)
    both = np.concatenate([np.cos(angle), -np.sin(angle)], axis=1) / math.sqrt(NFFT)
    return both.astype(np.float32).astype(jnp.bfloat16)


def position():
    inp, tim = lax.axis_index("inp"), lax.axis_index("tim")
    return (
        lax.div(inp, 16),
        lax.rem(lax.div(inp, 4), 4),
        lax.rem(inp, 4),
        lax.div(tim, 2),
        lax.rem(tim, 2),
    )


SIZES = (2, 4, 4, 2, 2)


def moved(place, by):
    z_lo, x, y, z_hi, core = [lax.rem(p + b, s) for p, b, s in zip(place, by, SIZES)]
    return z_lo * 16 + x * 4 + y, z_hi * 2 + core


AXES = {"x": 1, "y": 2, "z": 0}


def partners(axis):
    if axis == "tim":
        return [(0, 0, 0, a, b) for a in range(2) for b in range(2) if a or b]
    k = AXES[axis]
    return [tuple(s if q == k else 0 for q in range(5)) for s in range(1, SIZES[k])]


def spread(frames, v_hbm, w_ref, t_ref, recv, vbuf, filt, spec, turned, send,
           load_sem, halo_ssem, halo_rsem, ssem, rsem, stage_sem):
    inp, tim = lax.axis_index("inp"), lax.axis_index("tim")
    place = position()
    span = frames * NFFT
    halo = (TAPS - 1) * NFFT
    groups = frames // GROUP

    def load(half, g):
        cut = pl.ds(g * GROUP * NFFT, GROUP * NFFT)
        return pltpu.make_async_copy(
            v_hbm.at[pl.ds(half * ROWS, ROWS), cut], vbuf.at[half, :, cut], load_sem.at[half, g]
        )

    for half in range(2):
        for g in range(groups):
            load(half, g).start()

    barrier = pltpu.get_barrier_semaphore()
    near = [by for axis in ("tim", "x", "y", "z") for by in partners(axis)]
    for by in near:
        pl.semaphore_signal(barrier, inc=1, device_id=moved(place, by), device_id_type=MESH)

    def halo_copy(half):
        return pltpu.make_async_remote_copy(
            src_ref=v_hbm.at[pl.ds(half * ROWS, ROWS), pl.ds(0, halo)],
            dst_ref=vbuf.at[half, :, pl.ds(span, halo)],
            send_sem=halo_ssem.at[half],
            recv_sem=halo_rsem.at[half],
            device_id=(inp, lax.rem(tim + 3, 4)),
            device_id_type=MESH,
        )

    def filter_group(half, g):
        def lane_tile(j, carry):
            w = [w_ref[t, :, pl.ds(pl.multiple_of(j * LANES, LANES), LANES)] for t in range(TAPS)]

            def frame(f):
                at = pl.multiple_of(f * NFFT + j * LANES, LANES)
                return vbuf[half, :, pl.ds(at, LANES)].astype(jnp.float32)

            held = [frame(g * GROUP + t) for t in range(TAPS - 1)]
            for k in range(GROUP):
                held.append(frame(g * GROUP + k + TAPS - 1))
                total = (w[0] * held[k] + w[1] * held[k + 1]) + (w[2] * held[k + 2] + w[3] * held[k + 3])
                filt[pl.ds(g * GROUP * ROWS + k * ROWS, ROWS), pl.ds(pl.multiple_of(j * LANES, LANES), LANES)] = (
                    total.astype(jnp.bfloat16)
                )
            return carry

        lax.fori_loop(0, NFFT // LANES, lane_tile, 0)

    def transform_group(g):
        rows = pl.ds(g * GROUP * ROWS, GROUP * ROWS)
        found = jnp.dot(filt[rows, :], t_ref[...], preferred_element_type=jnp.float32)
        for q in range(2 * CHAN // LANES):
            spec[q, rows, :] = found[:, q * LANES : (q + 1) * LANES]

    def turn():
        def one(i, carry):
            for block in range(CHAN // LANES):
                parts = [
                    spec[part * (CHAN // LANES) + block, pl.ds(i, frames, stride=ROWS), :]
                    for part in range(2)
                ]
                both = jnp.concatenate(parts, axis=0)
                turned[pl.ds(pl.multiple_of(i * CHAN + block * LANES, LANES), LANES), :] = both.T
            return carry

        lax.fori_loop(0, ROWS, one, 0)

    def slot(ref, half):
        return ref.at[:, tim, pl.ds(pl.multiple_of(inp * 32 + half * ROWS, ROWS), ROWS), :]

    def block_for(to_inp, to_tim, ch):
        c = (to_inp * 4 + to_tim) * 2 + ch
        return turned[pl.ds(c, ROWS, stride=CHAN), :].astype(jnp.bfloat16)

    def send_half(half):
        for ch in range(2):
            recv[ch, tim, pl.ds(pl.multiple_of(inp * 32 + half * ROWS, ROWS), ROWS), :] = block_for(inp, tim, ch)

        def one(r, carry):
            p = lax.rem(r * STRIDE, 128)
            by = (lax.rem(lax.div(p, 16), 2), lax.rem(p, 4), lax.rem(lax.div(p, 4), 4),
                  lax.rem(lax.div(p, 32), 2), lax.div(p, 64))
            to_inp, to_tim = moved(place, by)
            for ch in range(2):
                send[half, r - 1, ch] = block_for(to_inp, to_tim, ch)
            pltpu.make_async_remote_copy(
                src_ref=send.at[half, r - 1],
                dst_ref=slot(recv, half),
                send_sem=ssem,
                recv_sem=rsem,
                device_id=(to_inp, to_tim),
                device_id_type=MESH,
            ).start()
            return carry

        lax.fori_loop(1, 128, one, 0)

    def stage(n, axis):
        group = partners(axis)
        for by in group:
            pl.semaphore_signal(stage_sem.at[n], inc=1, device_id=moved(place, by), device_id_type=MESH)
        pl.semaphore_wait(stage_sem.at[n], len(group))

    for half in range(2):
        for g in range(groups - 1):
            if g == 0:
                load(half, 0).wait()
            load(half, g + 1).wait()
            filter_group(half, g)
            transform_group(g)
            if half == 0:
                if g == 0:
                    pl.semaphore_wait(barrier, len(near))

                    @pl.when(tim > 0)
                    def _():
                        halo_copy(0).start()
                        halo_copy(1).start()

                    stage(0, "x")
                elif g == 1:
                    stage(1, "y")
                elif g == 2:
                    stage(2, "z")

        @pl.when(tim < 3)
        def _():
            halo_copy(half).wait_recv()

        @pl.when(tim == 3)
        def _():
            vbuf[half, :, pl.ds(span, halo)] = jnp.zeros((ROWS, halo), jnp.bfloat16)

        filter_group(half, groups - 1)
        transform_group(groups - 1)
        turn()
        if half == 0:
            stage(3, "tim")
        send_half(half)

    @pl.when(tim > 0)
    def _():
        halo_copy(0).wait_send()
        halo_copy(1).wait_send()

    everything = send.at[:, pl.ds(0, 127)]
    pltpu.make_async_copy(everything, everything, ssem).wait()
    pltpu.make_async_copy(everything, everything, rsem).wait()


def channelize(voltages, window, tab):
    inputs, samples = voltages.shape
    frames = samples // NFFT
    groups = frames // GROUP
    vmem = pl.BlockSpec(memory_space=pltpu.VMEM)
    return pl.pallas_call(
        functools.partial(spread, frames),
        out_shape=jax.ShapeDtypeStruct((2, 4, 1024, LANES), jnp.bfloat16),
        in_specs=[pl.BlockSpec(memory_space=pl.ANY), vmem, vmem],
        out_specs=vmem,
        scratch_shapes=[
            pltpu.VMEM((2, ROWS, samples + (TAPS - 1) * NFFT), jnp.bfloat16),
            pltpu.VMEM((frames * ROWS, NFFT), jnp.bfloat16),
            pltpu.VMEM((2 * CHAN // LANES, frames * ROWS, LANES), jnp.float32),
            pltpu.VMEM((ROWS * CHAN, LANES), jnp.float32),
            pltpu.VMEM((2, 128, 2, ROWS, LANES), jnp.bfloat16),
            pltpu.SemaphoreType.DMA((2, groups)),
            pltpu.SemaphoreType.DMA((2,)),
            pltpu.SemaphoreType.DMA((2,)),
            pltpu.SemaphoreType.DMA,
            pltpu.SemaphoreType.DMA,
            pltpu.SemaphoreType.REGULAR((4,)),
        ],
        compiler_params=pltpu.CompilerParams(
            collective_id=0, has_side_effects=True, vmem_limit_bytes=50 << 20
        ),
        name="channelize",
    )(voltages, window, tab)


def correlate_kernel(scale, rows, x_ref, o_ref):
    step = pl.program_id(1)
    own = pl.ds(pl.multiple_of(step * rows, rows), rows)
    every = jnp.concatenate([x_ref[0, b] for b in range(4)], axis=1)
    mine = [x_ref[0, b, own, :] for b in range(4)]
    half = LANES // 2
    turned = [jnp.concatenate([m[:, half:], -m[:, :half]], axis=1) for m in mine]
    dims = (((1,), (1,)), ((), ()))
    for part, lhs in enumerate((mine, turned)):
        o_ref[0, part] = scale * lax.dot_general(
            jnp.concatenate(lhs, axis=1), every, dims, preferred_element_type=jnp.float32
        )


def correlate(x, scale):
    channels, blocks, inputs, lanes = x.shape
    rows = 256
    return pl.pallas_call(
        functools.partial(correlate_kernel, scale, rows),
        grid=(channels, inputs // rows),
        out_shape=jax.ShapeDtypeStruct((channels, 2, inputs, inputs), jnp.float32),
        in_specs=[pl.BlockSpec((1, blocks, inputs, lanes), lambda c, i: (c, 0, 0, 0))],
        out_specs=pl.BlockSpec((1, 2, rows, inputs), lambda c, i: (c, 0, i, 0)),
        compiler_params=pltpu.CompilerParams(vmem_limit_bytes=40 << 20),
        name="correlate",
    )(x)


def local(voltages):
    frames = voltages.shape[1] // NFFT
    window = np.broadcast_to(filter_window()[:, None, :], (TAPS, ROWS, NFFT))
    received = channelize(voltages, jnp.asarray(window), jnp.asarray(table()))
    return correlate(received, 1.0 / (frames * lax.axis_size("tim")))


def solution(mesh):
    return jax.shard_map(
        local,
        mesh=mesh,
        in_specs=(P("inp", "tim"),),
        out_specs=P(("inp", "tim"), None, None, None),
        check_vma=False,
    )
```

```python
import functools
import math

import jax
import jax.numpy as jnp
import numpy as np
from jax import lax
from jax.experimental import pallas as pl
from jax.experimental.pallas import tpu as pltpu
from jax.sharding import PartitionSpec as P

NFFT = 2048
TAPS = 4
CH0 = 384
CHAN = 256
MESH = pl.DeviceIdType.MESH
ROWS = 16
LANES = 128
GROUP = 16
STRIDE = 85
PITCH = 65
LEAD = 257
CORR_ROWS = 256


def filter_window():
    span = TAPS * NFFT
    places = np.arange(span).astype(np.float32)
    centred = (places - np.float32(span / 2) + np.float32(0.5)) / np.float32(NFFT)
    taper = 0.5 - 0.5 * np.cos(2.0 * math.pi * (places + 0.5) / span)
    return (np.sinc(centred.astype(np.float64)) * taper).astype(np.float32).reshape(TAPS, NFFT)


def table():
    samples = np.arange(NFFT)
    channels = CH0 + np.arange(CHAN)
    angle = (samples[:, None] * channels[None, :] % NFFT) * (2.0 * math.pi / NFFT)
    both = np.concatenate([np.cos(angle), -np.sin(angle)], axis=1) / math.sqrt(NFFT)
    return both.astype(np.float32).astype(jnp.bfloat16)


def position():
    inp, tim = lax.axis_index("inp"), lax.axis_index("tim")
    return (
        lax.div(inp, 16),
        lax.rem(lax.div(inp, 4), 4),
        lax.rem(inp, 4),
        lax.div(tim, 2),
        lax.rem(tim, 2),
    )


SIZES = (2, 4, 4, 2, 2)


def moved(place, by):
    z_lo, x, y, z_hi, core = [lax.rem(p + b, s) for p, b, s in zip(place, by, SIZES)]
    return z_lo * 16 + x * 4 + y, z_hi * 2 + core


def partners(axis):
    if axis == "column":
        return [(a, 0, 0, b, c) for a in range(2) for b in range(2) for c in range(2) if a or b or c]
    k = {"x": 1, "y": 2}[axis]
    return [tuple(s if q == k else 0 for q in range(5)) for s in range(1, 4)]


def spread(frames, v_hbm, w_hbm, t_hbm, recv, vbuf, w_ref, t_ref, filt, spec, turned, send,
           load_sem, const_sem, halo_ssem, halo_rsem, own_sem, ssem, rsem, stage_sem):
    inp, tim = lax.axis_index("inp"), lax.axis_index("tim")
    me = inp * 4 + tim
    place = position()
    span = frames * NFFT
    halo = (TAPS - 1) * NFFT
    groups = frames // GROUP

    def load(half, g):
        cut = pl.ds(g * GROUP * NFFT, GROUP * NFFT)
        return pltpu.make_async_copy(
            v_hbm.at[pl.ds(half * ROWS, ROWS), cut], vbuf.at[half, :, cut], load_sem.at[half, g]
        )

    load_w = pltpu.make_async_copy(w_hbm, w_ref, const_sem.at[0])
    load_t = pltpu.make_async_copy(t_hbm, t_ref, const_sem.at[1])
    load_w.start()
    for g in range(groups):
        load(0, g).start()
        if g == 1:
            load_t.start()

    barrier = pltpu.get_barrier_semaphore()
    near = [by for axis in ("column", "x", "y") for by in partners(axis)]
    for by in near:
        pl.semaphore_signal(barrier, inc=1, device_id=moved(place, by), device_id_type=MESH)

    def halo_copy(half):
        return pltpu.make_async_remote_copy(
            src_ref=v_hbm.at[pl.ds(half * ROWS, ROWS), pl.ds(0, halo)],
            dst_ref=vbuf.at[half, :, pl.ds(span, halo)],
            send_sem=halo_ssem.at[half],
            recv_sem=halo_rsem.at[half],
            device_id=(inp, lax.rem(tim + 3, 4)),
            device_id_type=MESH,
        )

    tiles = NFFT // LANES // 2

    def filter_group(half, g, side):
        for j in range(tiles):
            lane = pl.multiple_of((side * tiles + j) * LANES, LANES)
            w = [jnp.broadcast_to(w_ref[pl.ds(t, 1), pl.ds(lane, LANES)], (ROWS, LANES)) for t in range(TAPS)]

            def frame(f):
                at = pl.multiple_of((g * GROUP + f) * NFFT + lane, LANES)
                return vbuf[half, :, pl.ds(at, LANES)].astype(jnp.float32)

            held = [frame(t) for t in range(TAPS - 1)]
            for k in range(GROUP):
                held.append(frame(k + TAPS - 1))
                total = (w[0] * held[k] + w[1] * held[k + 1]) + (w[2] * held[k + 2] + w[3] * held[k + 3])
                rows = pl.ds(pl.multiple_of((g * GROUP + k) * ROWS, ROWS), ROWS)
                filt[rows, pl.ds(lane, LANES)] = total.astype(jnp.bfloat16)

    def product(g, side):
        rows = pl.ds(pl.multiple_of(g * GROUP * ROWS, GROUP * ROWS), GROUP * ROWS)
        cut = pl.ds(pl.multiple_of(side * CHAN, CHAN), CHAN)
        return jnp.dot(filt[rows, :], t_ref[:, cut], preferred_element_type=jnp.float32)

    def keep(g, side, found):
        for q in range(CHAN // LANES):
            for k in range(GROUP):
                for h in range(ROWS // 8):
                    at = h * 8 * PITCH + g * GROUP + k
                    spec[side * 2 + q, pl.ds(at, 8, stride=PITCH), :] = found[
                        k * ROWS + h * 8 : k * ROWS + h * 8 + 8, q * LANES : (q + 1) * LANES
                    ]

    def front(half, g, with_filter, with_product):
        def one(side, carry):
            if with_product:
                found = product(g - 1, side)
            if with_filter:
                filter_group(half, g, side)
            if with_product:
                keep(g - 1, side, found)
            return carry

        lax.fori_loop(0, 2, one, 0)

    def turn():
        def one(n, carry):
            for i in (n * 2, n * 2 + 1):
                for block in range(CHAN // LANES):
                    both = jnp.concatenate(
                        [spec[part * 2 + block, pl.ds(i * PITCH, frames), :] for part in range(2)], axis=0
                    )
                    turned[pl.ds(i * LEAD + block * LANES, LANES), :] = both.astype(jnp.bfloat16).T.astype(jnp.float32)
            return carry

        lax.fori_loop(0, ROWS // 2, one, 0)

    def pack(half):
        def one(n, carry):
            for k in range(4):
                for ch in range(2):
                    c = n * 8 + k * 2 + ch
                    send[half, n * 4 + k, ch] = turned[pl.ds(c, ROWS, stride=LEAD), :].astype(jnp.bfloat16)
            return carry

        lax.fori_loop(0, CHAN // 8, one, 0)

    def slot(half):
        return recv.at[:, tim, pl.ds(pl.multiple_of(inp * 32 + half * ROWS, ROWS), ROWS), :]

    def own_copy(half):
        return pltpu.make_async_copy(send.at[half, me], slot(half), own_sem.at[half])

    def send_to(half, r):
        p = lax.rem(r * STRIDE, 128)
        by = (lax.rem(lax.div(p, 16), 2), lax.rem(p, 4), lax.rem(lax.div(p, 4), 4),
              lax.rem(lax.div(p, 32), 2), lax.div(p, 64))
        to_inp, to_tim = moved(place, by)
        pltpu.make_async_remote_copy(
            src_ref=send.at[half, to_inp * 4 + to_tim],
            dst_ref=slot(half),
            send_sem=ssem,
            recv_sem=rsem,
            device_id=(to_inp, to_tim),
            device_id_type=MESH,
        ).start()

    def send_half(half):
        own_copy(half).start()

        def one(n, carry):
            for k in range(7):
                send_to(half, 1 + n * 7 + k)
            return carry

        lax.fori_loop(0, 18, one, 0)
        send_to(half, 127)

    def stage(n, axis):
        group = partners(axis)
        for by in group:
            pl.semaphore_signal(stage_sem.at[n], inc=1, device_id=moved(place, by), device_id_type=MESH)
        pl.semaphore_wait(stage_sem.at[n], len(group))

    for half in range(2):
        load(half, 0).wait()
        load(half, 1).wait()
        if half == 0:
            for g in range(groups):
                load(1, g).start()
            load_w.wait()
        front(half, 0, True, False)
        if half == 0:
            load_t.wait()
            pl.semaphore_wait(barrier, len(near))

            @pl.when(tim > 0)
            def _():
                halo_copy(0).start()
                halo_copy(1).start()

        load(half, 2).wait()
        front(half, 1, True, True)
        if half == 0:
            stage(0, "x")
        load(half, 3).wait()
        front(half, 2, True, True)

        @pl.when(tim < 3)
        def _():
            halo_copy(half).wait_recv()

        @pl.when(tim == 3)
        def _():
            vbuf[half, :, pl.ds(span, halo)] = jnp.zeros((ROWS, halo), jnp.bfloat16)

        front(half, 3, True, True)
        front(half, 4, False, True)
        turn()
        pack(half)
        if half == 0:
            stage(1, "y")
        send_half(half)

    @pl.when(tim > 0)
    def _():
        halo_copy(0).wait_send()
        halo_copy(1).wait_send()

    own_copy(0).wait()
    own_copy(1).wait()
    everything = send.at[:, pl.ds(0, 127)]
    pltpu.make_async_copy(everything, everything, ssem).wait()
    pltpu.make_async_copy(everything, everything, rsem).wait()


def channelize(voltages, window, tab):
    samples = voltages.shape[1]
    frames = samples // NFFT
    groups = frames // GROUP
    hbm = pl.BlockSpec(memory_space=pltpu.HBM)
    return pl.pallas_call(
        functools.partial(spread, frames),
        out_shape=jax.ShapeDtypeStruct((2, 4, 1024, LANES), jnp.bfloat16),
        in_specs=[hbm, hbm, hbm],
        out_specs=pl.BlockSpec(memory_space=pltpu.VMEM),
        scratch_shapes=[
            pltpu.VMEM((2, ROWS, samples + (TAPS - 1) * NFFT), jnp.bfloat16),
            pltpu.VMEM((TAPS, NFFT), jnp.float32),
            pltpu.VMEM((NFFT, 2 * CHAN), jnp.bfloat16),
            pltpu.VMEM((frames * ROWS, NFFT), jnp.bfloat16),
            pltpu.VMEM((2 * CHAN // LANES, ROWS * PITCH + 72, LANES), jnp.float32),
            pltpu.VMEM((ROWS * LEAD + 264, LANES), jnp.float32),
            pltpu.VMEM((2, 128, 2, ROWS, LANES), jnp.bfloat16),
            pltpu.SemaphoreType.DMA((2, groups)),
            pltpu.SemaphoreType.DMA((2,)),
            pltpu.SemaphoreType.DMA((2,)),
            pltpu.SemaphoreType.DMA((2,)),
            pltpu.SemaphoreType.DMA((2,)),
            pltpu.SemaphoreType.DMA,
            pltpu.SemaphoreType.DMA,
            pltpu.SemaphoreType.REGULAR((2,)),
        ],
        compiler_params=pltpu.CompilerParams(
            collective_id=0, has_side_effects=True, vmem_limit_bytes=50 << 20
        ),
        name="channelize",
    )(voltages, window, tab)


def correlate_kernel(scale, rows, x_ref, o_hbm, obuf, sem):
    channels, blocks, inputs, lanes = x_ref.shape
    half = lanes // 2
    dims = (((1,), (1,)), ((), ()))

    def copy(ch, n):
        own = pl.ds(n * rows, rows)
        return pltpu.make_async_copy(obuf.at[ch, :, own, :], o_hbm.at[ch, :, own, :], sem.at[ch, n])

    for ch in range(channels):
        for n in range(inputs // rows):
            every = jnp.concatenate([x_ref[ch, b] for b in range(blocks)], axis=1)
            own = pl.ds(n * rows, rows)
            mine = [x_ref[ch, b, own, :] for b in range(blocks)]
            swapped = [jnp.concatenate([m[:, half:], -m[:, :half]], axis=1) for m in mine]
            for part, lhs in enumerate((mine, swapped)):
                obuf[ch, part, own, :] = scale * lax.dot_general(
                    jnp.concatenate(lhs, axis=1), every, dims, preferred_element_type=jnp.float32
                )
            copy(ch, n).start()
    for ch in range(channels):
        for n in range(inputs // rows):
            copy(ch, n).wait()


def correlate(x, scale):
    channels, blocks, inputs, lanes = x.shape
    rows = CORR_ROWS
    shape = (channels, 2, inputs, inputs)
    return pl.pallas_call(
        functools.partial(correlate_kernel, scale, rows),
        out_shape=jax.ShapeDtypeStruct(shape, jnp.float32),
        in_specs=[pl.BlockSpec(memory_space=pltpu.VMEM)],
        out_specs=pl.BlockSpec(memory_space=pl.ANY),
        scratch_shapes=[
            pltpu.VMEM(shape, jnp.float32),
            pltpu.SemaphoreType.DMA((channels, inputs // rows)),
        ],
        compiler_params=pltpu.CompilerParams(vmem_limit_bytes=40 << 20),
        name="correlate",
    )(x)


def local(voltages):
    frames = voltages.shape[1] // NFFT
    received = channelize(voltages, jnp.asarray(filter_window()), jnp.asarray(table()))
    return correlate(received, 1.0 / (frames * lax.axis_size("tim")))


def solution(mesh):
    return jax.shard_map(
        local,
        mesh=mesh,
        in_specs=(P("inp", "tim"),),
        out_specs=P(("inp", "tim"), None, None, None),
        check_vma=False,
    )
```

```python
import functools
import math

import jax
import jax.numpy as jnp
import numpy as np
from jax import lax
from jax.experimental import pallas as pl
from jax.experimental.pallas import tpu as pltpu
from jax.sharding import PartitionSpec as P

NFFT = 2048
TAPS = 4
CH0 = 384
CHAN = 256
MESH = pl.DeviceIdType.MESH
ROWS = 16
LANES = 128
GROUP = 16
STRIDE = 85
PITCH = 65
LEAD = 257
CORR_ROWS = 256
WINDOW_ROWS = 3 * TAPS * NFFT // (2 * CHAN)


def filter_window():
    span = TAPS * NFFT
    places = np.arange(span).astype(np.float32)
    centred = (places - np.float32(span / 2) + np.float32(0.5)) / np.float32(NFFT)
    taper = 0.5 - 0.5 * np.cos(2.0 * math.pi * (places + 0.5) / span)
    return (np.sinc(centred.astype(np.float64)) * taper).astype(np.float32).reshape(TAPS, NFFT)


def table():
    samples = np.arange(NFFT)
    channels = CH0 + np.arange(CHAN)
    angle = (samples[:, None] * channels[None, :] % NFFT) * (2.0 * math.pi / NFFT)
    both = np.concatenate([np.cos(angle), -np.sin(angle)], axis=1) / math.sqrt(NFFT)
    rest, terms = filter_window(), []
    for _ in range(3):
        terms.append(rest.astype(jnp.bfloat16))
        rest = rest - terms[-1].astype(np.float32)
    terms = np.stack(terms).reshape(WINDOW_ROWS, 2 * CHAN)
    return np.concatenate([both.astype(np.float32).astype(jnp.bfloat16), terms], axis=0)


def position():
    inp, tim = lax.axis_index("inp"), lax.axis_index("tim")
    return (
        lax.div(inp, 16),
        lax.rem(lax.div(inp, 4), 4),
        lax.rem(inp, 4),
        lax.div(tim, 2),
        lax.rem(tim, 2),
    )


SIZES = (2, 4, 4, 2, 2)


def moved(place, by):
    z_lo, x, y, z_hi, core = [lax.rem(p + b, s) for p, b, s in zip(place, by, SIZES)]
    return z_lo * 16 + x * 4 + y, z_hi * 2 + core


def partners(axis):
    if axis == "column":
        return [(a, 0, 0, b, c) for a in range(2) for b in range(2) for c in range(2) if a or b or c]
    k = {"x": 1, "y": 2}[axis]
    return [tuple(s if q == k else 0 for q in range(5)) for s in range(1, 4)]


def spread(frames, v_hbm, t_hbm, recv, vbuf, w_ref, wt_ref, t_ref, filt, spec, turned, send,
           load_sem, const_sem, halo_ssem, halo_rsem, own_sem, ssem, rsem, stage_sem):
    inp, tim = lax.axis_index("inp"), lax.axis_index("tim")
    me = inp * 4 + tim
    place = position()
    span = frames * NFFT
    halo = (TAPS - 1) * NFFT
    groups = frames // GROUP

    def load(half, g):
        first = g * GROUP + (TAPS - 1 if g else 0)
        last = (g + 1) * GROUP + TAPS - 1 if g < groups - 1 else frames
        cut = pl.ds(first * NFFT, (last - first) * NFFT)
        return pltpu.make_async_copy(
            v_hbm.at[pl.ds(half * ROWS, ROWS), cut], vbuf.at[half, :, cut], load_sem.at[half, g]
        )

    load_w = pltpu.make_async_copy(t_hbm.at[pl.ds(NFFT, WINDOW_ROWS)], wt_ref, const_sem.at[0])
    load_t = pltpu.make_async_copy(t_hbm.at[pl.ds(0, NFFT)], t_ref, const_sem.at[1])
    load_w.start()
    for g in range(groups):
        load(0, g).start()
        if g == 0:
            load_t.start()

    barrier = pltpu.get_barrier_semaphore()
    near = [by for axis in ("column", "x", "y") for by in partners(axis)]
    for by in near:
        pl.semaphore_signal(barrier, inc=1, device_id=moved(place, by), device_id_type=MESH)

    def halo_copy(half):
        return pltpu.make_async_remote_copy(
            src_ref=v_hbm.at[pl.ds(half * ROWS, ROWS), pl.ds(0, halo)],
            dst_ref=vbuf.at[half, :, pl.ds(span, halo)],
            send_sem=halo_ssem.at[half],
            recv_sem=halo_rsem.at[half],
            device_id=(inp, lax.rem(tim + 3, 4)),
            device_id_type=MESH,
        )

    tiles = NFFT // LANES // 2

    def window():
        per = NFFT // (2 * CHAN)
        for t in range(TAPS):
            for q in range(per):
                terms = [wt_ref[pl.ds((k * TAPS + t) * per + q, 1), :].astype(jnp.float32) for k in range(3)]
                w_ref[pl.ds(t, 1), pl.ds(q * 2 * CHAN, 2 * CHAN)] = (terms[0] + terms[1]) + terms[2]

    def filter_group(half, g, side):
        for j in range(tiles):
            lane = pl.multiple_of((side * tiles + j) * LANES, LANES)
            w = [jnp.broadcast_to(w_ref[pl.ds(t, 1), pl.ds(lane, LANES)], (ROWS, LANES)) for t in range(TAPS)]

            def frame(f):
                at = pl.multiple_of((g * GROUP + f) * NFFT + lane, LANES)
                return vbuf[half, :, pl.ds(at, LANES)].astype(jnp.float32)

            held = [frame(t) for t in range(TAPS - 1)]
            for k in range(GROUP):
                held.append(frame(k + TAPS - 1))
                total = (w[0] * held[k] + w[1] * held[k + 1]) + (w[2] * held[k + 2] + w[3] * held[k + 3])
                rows = pl.ds(pl.multiple_of((g * GROUP + k) * ROWS, ROWS), ROWS)
                filt[rows, pl.ds(lane, LANES)] = total.astype(jnp.bfloat16)

    def product(g, side):
        rows = pl.ds(pl.multiple_of(g * GROUP * ROWS, GROUP * ROWS), GROUP * ROWS)
        cut = pl.ds(pl.multiple_of(side * CHAN, CHAN), CHAN)
        return jnp.dot(filt[rows, :], t_ref[:, cut], preferred_element_type=jnp.float32)

    def keep(g, side, found):
        for q in range(CHAN // LANES):
            for k in range(GROUP):
                for h in range(ROWS // 8):
                    at = h * 8 * PITCH + g * GROUP + k
                    spec[side * 2 + q, pl.ds(at, 8, stride=PITCH), :] = found[
                        k * ROWS + h * 8 : k * ROWS + h * 8 + 8, q * LANES : (q + 1) * LANES
                    ]

    def front(half, g, with_filter, with_product):
        def one(side, carry):
            if with_product:
                found = product(g - 1, side)
            if with_filter:
                filter_group(half, g, side)
            if with_product:
                keep(g - 1, side, found)
            return carry

        lax.fori_loop(0, 2, one, 0)

    def turn():
        def one(n, carry):
            for i in (n * 2, n * 2 + 1):
                for block in range(CHAN // LANES):
                    both = jnp.concatenate(
                        [spec[part * 2 + block, pl.ds(i * PITCH, frames), :] for part in range(2)], axis=0
                    )
                    turned[pl.ds(i * LEAD + block * LANES, LANES), :] = both.astype(jnp.bfloat16).T.astype(jnp.float32)
            return carry

        lax.fori_loop(0, ROWS // 2, one, 0)

    def pack(half):
        def one(n, carry):
            for k in range(4):
                for ch in range(2):
                    c = n * 8 + k * 2 + ch
                    send[half, n * 4 + k, ch] = turned[pl.ds(c, ROWS, stride=LEAD), :].astype(jnp.bfloat16)
            return carry

        lax.fori_loop(0, CHAN // 8, one, 0)

    def slot(half):
        return recv.at[tim, inp, half]

    def own_copy(half):
        return pltpu.make_async_copy(send.at[half, me], slot(half), own_sem.at[half])

    def send_to(half, r):
        p = lax.rem(r * STRIDE, 128)
        by = (lax.rem(lax.div(p, 16), 2), lax.rem(p, 4), lax.rem(lax.div(p, 4), 4),
              lax.rem(lax.div(p, 32), 2), lax.div(p, 64))
        to_inp, to_tim = moved(place, by)
        pltpu.make_async_remote_copy(
            src_ref=send.at[half, to_inp * 4 + to_tim],
            dst_ref=slot(half),
            send_sem=ssem,
            recv_sem=rsem,
            device_id=(to_inp, to_tim),
            device_id_type=MESH,
        ).start()

    def send_half(half):
        own_copy(half).start()

        def one(n, carry):
            for k in range(7):
                send_to(half, 1 + n * 7 + k)
            return carry

        lax.fori_loop(0, 18, one, 0)
        send_to(half, 127)

    def tell(n, axis):
        for by in partners(axis):
            pl.semaphore_signal(stage_sem.at[n], inc=1, device_id=moved(place, by), device_id_type=MESH)

    def hear(n, axis):
        pl.semaphore_wait(stage_sem.at[n], len(partners(axis)))

    for half in range(2):
        if half == 0:
            load_w.wait()
            window()
        load(half, 0).wait()
        front(half, 0, True, False)
        if half == 0:
            for g in range(groups):
                load(1, g).start()
            load_t.wait()
            pl.semaphore_wait(barrier, len(near))

            @pl.when(tim > 0)
            def _():
                halo_copy(0).start()
                halo_copy(1).start()

            tell(0, "x")
        load(half, 1).wait()
        front(half, 1, True, True)
        load(half, 2).wait()
        front(half, 2, True, True)
        load(half, 3).wait()
        if half == 0:
            hear(0, "x")
            tell(1, "y")

        @pl.when(tim < 3)
        def _():
            halo_copy(half).wait_recv()

        @pl.when(tim == 3)
        def _():
            vbuf[half, :, pl.ds(span, halo)] = jnp.zeros((ROWS, halo), jnp.bfloat16)

        front(half, 3, True, True)
        front(half, 4, False, True)
        turn()
        pack(half)
        if half == 0:
            hear(1, "y")
        send_half(half)

    @pl.when(tim > 0)
    def _():
        halo_copy(0).wait_send()
        halo_copy(1).wait_send()

    own_copy(0).wait()
    own_copy(1).wait()
    everything = send.at[:, pl.ds(0, 127)]
    pltpu.make_async_copy(everything, everything, ssem).wait()
    pltpu.make_async_copy(everything, everything, rsem).wait()


def channelize(voltages, tab):
    samples = voltages.shape[1]
    frames = samples // NFFT
    groups = frames // GROUP
    hbm = pl.BlockSpec(memory_space=pltpu.HBM)
    return pl.pallas_call(
        functools.partial(spread, frames),
        out_shape=jax.ShapeDtypeStruct((4, 32, 2, 2, ROWS, LANES), jnp.bfloat16),
        in_specs=[hbm, hbm],
        out_specs=pl.BlockSpec(memory_space=pltpu.VMEM),
        scratch_shapes=[
            pltpu.VMEM((2, ROWS, samples + (TAPS - 1) * NFFT), jnp.bfloat16),
            pltpu.VMEM((TAPS, NFFT), jnp.float32),
            pltpu.VMEM((WINDOW_ROWS, 2 * CHAN), jnp.bfloat16),
            pltpu.VMEM((NFFT, 2 * CHAN), jnp.bfloat16),
            pltpu.VMEM((frames * ROWS, NFFT), jnp.bfloat16),
            pltpu.VMEM((2 * CHAN // LANES, ROWS * PITCH + 72, LANES), jnp.float32),
            pltpu.VMEM((ROWS * LEAD + 264, LANES), jnp.float32),
            pltpu.VMEM((2, 128, 2, ROWS, LANES), jnp.bfloat16),
            pltpu.SemaphoreType.DMA((2, groups)),
            pltpu.SemaphoreType.DMA((2,)),
            pltpu.SemaphoreType.DMA((2,)),
            pltpu.SemaphoreType.DMA((2,)),
            pltpu.SemaphoreType.DMA((2,)),
            pltpu.SemaphoreType.DMA,
            pltpu.SemaphoreType.DMA,
            pltpu.SemaphoreType.REGULAR((2,)),
        ],
        compiler_params=pltpu.CompilerParams(
            collective_id=0, has_side_effects=True, vmem_limit_bytes=50 << 20
        ),
        name="channelize",
    )(voltages, tab)


def correlate_kernel(scale, rows, x_ref, o_hbm, obuf, sem):
    blocks, sources, halves, channels, _, lanes = x_ref.shape
    inputs = o_hbm.shape[-1]
    half = lanes // 2
    per = inputs // sources
    dims = (((1,), (1,)), ((), ()))

    def copy(ch, n):
        own = pl.ds(n * rows, rows)
        return pltpu.make_async_copy(obuf.at[ch, :, own, :], o_hbm.at[ch, :, own, :], sem.at[ch, n])

    for ch in range(channels):
        for n in range(inputs // rows):
            every = jnp.concatenate([x_ref[b, :, :, ch].reshape(inputs, lanes) for b in range(blocks)], axis=1)
            own = pl.ds(n * rows, rows)
            mine = [x_ref[b, pl.ds(n * rows // per, rows // per), :, ch].reshape(rows, lanes) for b in range(blocks)]
            swapped = [jnp.concatenate([m[:, half:], -m[:, :half]], axis=1) for m in mine]
            for part, lhs in enumerate((mine, swapped)):
                obuf[ch, part, own, :] = scale * lax.dot_general(
                    jnp.concatenate(lhs, axis=1), every, dims, preferred_element_type=jnp.float32
                )
            copy(ch, n).start()
    for ch in range(channels):
        for n in range(inputs // rows):
            copy(ch, n).wait()


def correlate(x, scale):
    _, sources, halves, channels, part_rows, _ = x.shape
    inputs = sources * halves * part_rows
    rows = CORR_ROWS
    shape = (channels, 2, inputs, inputs)
    return pl.pallas_call(
        functools.partial(correlate_kernel, scale, rows),
        out_shape=jax.ShapeDtypeStruct(shape, jnp.float32),
        in_specs=[pl.BlockSpec(memory_space=pltpu.VMEM)],
        out_specs=pl.BlockSpec(memory_space=pl.ANY),
        scratch_shapes=[
            pltpu.VMEM(shape, jnp.float32),
            pltpu.SemaphoreType.DMA((channels, inputs // rows)),
        ],
        compiler_params=pltpu.CompilerParams(vmem_limit_bytes=40 << 20),
        name="correlate",
    )(x)


def local(voltages):
    frames = voltages.shape[1] // NFFT
    received = channelize(voltages, jnp.asarray(table()))
    return correlate(received, 1.0 / (frames * lax.axis_size("tim")))


def solution(mesh):
    return jax.shard_map(
        local,
        mesh=mesh,
        in_specs=(P("inp", "tim"),),
        out_specs=P(("inp", "tim"), None, None, None),
        check_vma=False,
    )
```
